32 devices in a mesh: ctx: 16 (over z, y, x), head: 2 (over core).
Axes of the slice: x: 2, y: 2, z: 4, core: 2. Of those that a mesh axis runs over, the one named last changes fastest.
Arguments:
- q_nope: bfloat16 [4096, 8192], P('ctx', 'head'), may hold values from -6 to 6
- q_rope: bfloat16 [4096, 4096], P('ctx', 'head'), may hold values from -64 to 64
- latents: bfloat16 [4096, 512], P(('ctx', 'head')), may hold values from -6 to 6
- rope_keys: bfloat16 [64, 4096], P(None, ('ctx', 'head')), may hold values from -4 to 4
- doc_lengths: int32 [8], replicated, may hold values from 1 to 1792, 4096 in all
- w_key: bfloat16 [512, 8192], P(None, 'head'), may hold values from -0.25 to 0.25
- w_value: bfloat16 [512, 8192], P(None, 'head'), may hold values from -0.25 to 0.25
Outputs:
- attended: bfloat16 [4096, 8192], P('ctx', 'head')
The draws below stay inside these ranges and needn't reach their ends.
Inputs may be any that keep to these rules, and one draw needn't show every extreme that they name: `doc_lengths`: they sum to 4096.
All inputs are finite; a program needn't handle non-finite values.
Results may differ from the reference program's by a relative error of at most 0.0064.
Values may be sent and summed in bfloat16 or wider, within the bound.
No kernel may reach another device: no remote copies, remote signals or barrier semaphores. Data moves between devices by JAX's collectives and lax.ppermute only.
A program may use at most 256 MiB of HBM per device.

```python
import math
import jax
import jax.numpy as jnp
import numpy as np
from jax import lax

HEADS = 64
HEAD_DIM = 128
ROPE = 64
LATENT = 512
WINDOW = 8
TOK_DEV = 256
TOKENS = 4096
DOCS = 8
DOC_MOST = 1792


def draw_rope_keys(key, part):
    own_key = jax.random.fold_in(key, 5)
    rows_out = jax.random.truncated_normal(own_key, -4.0, 4.0, (TOKENS, ROPE), jnp.float32)
    return rows_out.T.astype(jnp.bfloat16)


def draw_q_rope(key, part):
    own_key = jax.random.fold_in(key, 7)
    rows_out = jax.random.truncated_normal(own_key, -4.0, 4.0, (TOKENS, HEADS * ROPE), jnp.float32)
    return rows_out.astype(jnp.bfloat16)


def shard_levels(key, extent, pieces, low, largest):
    factor_of, own = 1.0, jax.random.fold_in(key, 6)
    for axis_at, shards_of in pieces:
        heights = jnp.exp(jax.random.uniform(jax.random.fold_in(own, axis_at), (shards_of,), jnp.float32, low / len(pieces), largest / len(pieces)))
        factor_of = factor_of * jnp.repeat(heights, extent[axis_at] // shards_of).reshape([-1 if axis == axis_at else 1 for axis in range(len(extent))])
    return factor_of


def profile(number_of, total, limit, slope):
    portions = [(1 << 20) // math.isqrt(standing ** slope) + 1 for standing in range(2, number_of + 1)]
    surplus, counts = total - limit - (number_of - 1), [1] * (number_of - 1)
    while surplus > 0:
        free = [i for i in range(number_of - 1) if counts[i] < limit]
        pool, left = sum([portions[i] for i in free]), surplus
        for i in free:
            addition = min(limit - counts[i], max(1, left * portions[i] // pool), surplus)
            counts[i] = counts[i] + addition
            surplus = surplus - addition
    return np.array([limit] + counts)


def ragged_sizes(key, amount, total, bound, lean):
    if amount == 2:
        one = jax.random.randint(key, (), max(1, total - bound), min(bound, total - 1) + 1)
        return jnp.stack([one, total - one])
    sizes = jnp.asarray(profile(amount, total, bound, lean), jnp.int32)
    couples = (amount - 1) // 2
    donor, taker = sizes[1:1 + 2 * couples:2], sizes[2:2 + 2 * couples:2]
    margin = jnp.minimum(donor - 1, bound - taker)
    moved = jax.random.randint(jax.random.fold_in(key, 1), (couples,), 0, 1 << 20) % (margin + 1)
    sizes = sizes.at[1:1 + 2 * couples:2].set(donor - moved).at[2:2 + 2 * couples:2].set(taker + moved)
    return sizes[jax.random.permutation(jax.random.fold_in(key, 2), amount)]


def centred(key, extent, scale, bound, shards=(), kind=jnp.bfloat16):
    values = scale * jax.random.normal(key, extent, jnp.float32)
    if shards:
        values = values * shard_levels(key, extent, shards, -0.22, 0.18)
    return jnp.clip(values, -bound, bound).astype(kind)


def setup_inputs(seed: int = 0) -> dict:
    splits = jax.random.split(jax.random.key(seed), 8)
    q_nope = centred(splits[0], (TOKENS, HEADS * HEAD_DIM), 1.0, 6.0, ((0, 16), (1, 2)))
    q_rope = draw_q_rope(jax.random.fold_in(splits[7], 71), 0)
    latents = centred(splits[2], (TOKENS, LATENT), 1.0, 6.0, ((0, 32),))
    rope_keys = draw_rope_keys(jax.random.fold_in(splits[7], 71), 0)
    doc_lengths = ragged_sizes(splits[4], DOCS, TOKENS, DOC_MOST, 1).astype(jnp.int32)
    w_key = centred(splits[5], (LATENT, HEADS * HEAD_DIM), LATENT ** -0.5, 0.25, ((1, 2),))
    w_value = centred(splits[6], (LATENT, HEADS * HEAD_DIM), LATENT ** -0.5, 0.25, ((1, 2),))
    return {"q_nope": q_nope, "q_rope": q_rope, "latents": latents, "rope_keys": rope_keys, "doc_lengths": doc_lengths, "w_key": w_key, "w_value": w_value}


def segment_of(positions, doc_starts):
    return lax.optimization_barrier(jnp.sum((doc_starts[None, :] <= positions[:, None]).astype(jnp.int32), axis=1)) - 1

def reference(q_nope, q_rope, latents, rope_keys, doc_lengths, w_key, w_value):
    doc_starts = (jnp.cumsum(doc_lengths) - doc_lengths).astype(jnp.int32)
    key_nope = jnp.dot(latents, w_key, preferred_element_type=jnp.float32).astype(jnp.bfloat16)
    values = jnp.dot(latents, w_value, preferred_element_type=jnp.float32).astype(jnp.bfloat16)
    span_rows = WINDOW * TOK_DEV
    back_rows = span_rows - TOK_DEV
    key_padded = jnp.concatenate([jnp.zeros((back_rows, key_nope.shape[1]), jnp.bfloat16), key_nope], 0)
    value_padded = jnp.concatenate([jnp.zeros((back_rows, values.shape[1]), jnp.bfloat16), values], 0)
    rope_padded = jnp.concatenate([jnp.zeros((ROPE, back_rows), jnp.bfloat16), rope_keys], 1)
    score_scale = 1.0 / math.sqrt(HEAD_DIM + ROPE)

    def one_block(block_index):
        first_row = (block_index * TOK_DEV).astype(jnp.int32)
        query_nope = lax.dynamic_slice_in_dim(q_nope, first_row, TOK_DEV, 0).reshape(TOK_DEV, HEADS, HEAD_DIM)
        query_rope = lax.dynamic_slice_in_dim(q_rope, first_row, TOK_DEV, 0).reshape(TOK_DEV, HEADS, ROPE)
        key_block = lax.dynamic_slice_in_dim(key_padded, first_row, span_rows, 0).reshape(span_rows, HEADS, HEAD_DIM)
        value_block = lax.dynamic_slice_in_dim(value_padded, first_row, span_rows, 0).reshape(span_rows, HEADS, HEAD_DIM)
        rope_block = lax.dynamic_slice_in_dim(rope_padded, first_row, span_rows, 1)
        query_place = first_row + jnp.arange(TOK_DEV, dtype=jnp.int32)
        key_place = first_row - back_rows + jnp.arange(span_rows, dtype=jnp.int32)
        visible = (segment_of(key_place, doc_starts)[None, :] == segment_of(query_place, doc_starts)[:, None]) & (key_place[None, :] <= query_place[:, None])
        scores = jnp.einsum('qhd,khd->qhk', query_nope.astype(jnp.float32), key_block.astype(jnp.float32))
        scores = scores + jnp.einsum('qhr,rk->qhk', query_rope.astype(jnp.float32), rope_block.astype(jnp.float32))
        scores = scores * score_scale
        scores = jnp.where(visible[:, None, :], scores, jnp.float32(-1e+30))
        row_top = lax.optimization_barrier(jnp.max(scores, axis=2, keepdims=True))
        raised = jnp.exp(scores - row_top)
        denom_sum = lax.optimization_barrier(jnp.sum(raised, axis=2))
        weights = raised.astype(jnp.bfloat16)
        mixed_sum = jnp.einsum('qhk,khd->qhd', weights.astype(jnp.float32), value_block.astype(jnp.float32))
        return (mixed_sum / denom_sum[:, :, None]).astype(jnp.bfloat16).reshape(TOK_DEV, HEADS * HEAD_DIM)
    block_count = TOKENS // TOK_DEV
    result = lax.map(one_block, jnp.arange(block_count, dtype=jnp.int32))
    return result.reshape(TOKENS, HEADS * HEAD_DIM)
```

```python
import functools
import math

import jax
import jax.numpy as jnp
from jax import lax
from jax.experimental import pallas as pl
from jax.experimental.pallas import tpu as pltpu
from jax.sharding import PartitionSpec as P

HEAD_DIM = 128
WINDOW = 8
GROUP = 4

masked_score = -1e30
f32, bf16 = jnp.float32, jnp.bfloat16
NT = (((1,), (1,)), ((), ()))


def from_behind(x, by):
    length = lax.axis_size("ctx")
    return lax.ppermute(x, "ctx", [(i, (i + by) % length) for i in range(length)])


def pack_kernel(latents, rope_keys, packed):
    rows = latents.shape[0]
    packed[:rows, :] = latents[...]
    lanes = rope_keys.shape[1]
    pieces = latents.shape[1] // lanes
    tall = rope_keys.shape[0] // pieces
    for piece in range(pieces):
        packed[rows:, piece * lanes : (piece + 1) * lanes] = rope_keys[
            piece * tall : (piece + 1) * tall, :
        ]


def pack(latents, rope_keys):
    rows, width = latents.shape
    below = rope_keys.size // width
    return pl.pallas_call(
        pack_kernel, out_shape=jax.ShapeDtypeStruct((rows + below, width), bf16)
    )(latents, rope_keys)


def attend_kernel(shape, *refs):
    blocks, parts, first_back, first, last, rope = shape
    lengths, place = refs[:2]
    material = refs[2 : 2 + parts]
    q_nope, q_rope, w_key, w_value = refs[2 + parts : 6 + parts]
    rest = refs[6 + parts :]
    if not first:
        acc_in, stat_in = rest[:2]
        rest = rest[2:]
    if last:
        out = rest[0]
        rest = rest[1:]
    else:
        acc_out, stat_out = rest[:2]
        rest = rest[2:]
    keys, values, side, query_side, *score_and_weight = rest
    score_refs, weight_refs = score_and_weight[:2], score_and_weight[2:]
    tok = q_nope.shape[0]
    span = blocks * tok
    part_rows = tok // parts
    width = w_key.shape[0]
    scale = math.log2(math.e) / math.sqrt(HEAD_DIM + rope)
    lane = lax.broadcasted_iota(jnp.int32, (tok, 128), 1)
    low = lane < 64

    @pl.when(pl.program_id(0) == 0)
    def _():
        at = lax.broadcasted_iota(jnp.int32, (8, 128), 1) % 64
        start, stop = jnp.zeros((8, 128), jnp.int32), jnp.zeros((8, 128), jnp.int32)
        before = jnp.int32(0)
        for doc in range(lengths.shape[0]):
            after = before + lengths[doc]
            start = jnp.where(at == doc, before, start)
            stop = jnp.where(at == doc, after, stop)
            before = after
        start, stop = start[:1], stop[:1]
        row = lax.broadcasted_iota(jnp.int32, (tok, 128), 0)
        position = place[0] * tok + row
        inside = (position >= start) & (position < stop)
        query_side[...] = jnp.where(inside, 1.0, 0.0).astype(bf16)
        for block in range(blocks):
            position = (place[0] - first_back - block) * tok + (row + place[1] * part_rows) % tok
            inside = (position >= start) & (position < stop)
            other = jnp.where(inside, 0.0, masked_score)
            rotary = []
            for part in range(parts):
                folded = material[part][block, part_rows:, :].astype(f32)
                pieces = width // part_rows
                flat = jnp.concatenate(
                    [folded[:, p * part_rows : (p + 1) * part_rows] for p in range(pieces)], axis=0
                )
                flat = jnp.concatenate([flat, flat], axis=0)
                rotary.append(flat.T)
            rotary = jnp.concatenate(rotary, axis=0)
            rows = slice(block * tok, (block + 1) * tok)
            side[0, rows, :] = jnp.where(low, rotary, other).astype(bf16)
            side[1, rows, :] = jnp.where(low, other, rotary).astype(bf16)

    def latents(block):
        return jnp.concatenate([m[block, :part_rows, :] for m in material], axis=0)

    held = {}

    def project(into, weight, pair, block):
        rows, columns = slice(block * tok, (block + 1) * tok), slice(pair * 256, (pair + 1) * 256)
        into[rows, columns] = jnp.dot(
            latents(block), weight[:, columns], preferred_element_type=f32
        ).astype(bf16)

    def score(head, block):
        rows = slice(block * tok, (block + 1) * tok)
        columns = slice(head * HEAD_DIM, (head + 1) * HEAD_DIM)
        pair, odd = divmod(head, 2)
        if block == 0:
            rotary = q_rope[:, pair * 128 : (pair + 1) * 128]
            held["query", head] = jnp.concatenate(
                [q_nope[:, columns], jnp.where(low != (odd == 1), rotary, query_side[...])], axis=1
            )
        key = jnp.concatenate([keys[rows, columns], side[odd, rows, :]], axis=1)
        scores = lax.dot_general(held["query", head], key, NT, preferred_element_type=f32)
        if first_back + block == 0:
            query_at = lax.broadcasted_iota(jnp.int32, (tok, tok), 0)
            key_at = lax.broadcasted_iota(jnp.int32, (tok, tok), 1)
            key_at = (key_at + place[1] * part_rows) % tok
            scores = jnp.where(key_at <= query_at, scores, masked_score)
        score_refs[head % 2][:, rows] = scores
        top = jnp.maximum(scores[:, :128], scores[:, 128:])
        held["top", head] = top if block == 0 else jnp.maximum(held["top", head], top)
        if block == blocks - 1:
            top = jnp.max(held["top", head], axis=1, keepdims=True) * scale
            if not first:
                earlier = stat_in[0, :, head : head + 1]
                top = jnp.maximum(top, earlier)
                held["fade", head] = jnp.exp2(earlier - top)
            held["top", head] = top

    def raise_(head, block):
        rows = slice(block * tok, (block + 1) * tok)
        raised = jnp.exp2(score_refs[head % 2][:, rows] * scale - held["top", head])
        weight_refs[head % 2][:, rows] = raised.astype(bf16)

    def mix(head):
        columns = slice(head * HEAD_DIM, (head + 1) * HEAD_DIM)
        value = jnp.concatenate([values[:, columns], jnp.ones((span, 128), bf16)], axis=1)
        mixed = jnp.dot(weight_refs[head % 2][...], value, preferred_element_type=f32)
        mixed, denom = mixed[:, :128], mixed[:, 128:]
        if not first:
            mixed = mixed + acc_in[:, columns] * held["fade", head]
            denom = denom + stat_in[0, :, GROUP + head : GROUP + head + 1] * held["fade", head]
        if last:
            out[:, columns] = (mixed / denom).astype(bf16)
        else:
            acc_out[:, columns] = mixed
            stat_out[0, :, head : head + 1] = held["top", head]
            stat_out[0, :, GROUP + head : GROUP + head + 1] = denom[:, :1]

    def together(*lists):
        for at in range(max(map(len, lists))):
            for each in lists:
                if at < len(each):
                    each[at]()

    def over(call, *args):
        return [functools.partial(call, *args, block) for block in range(blocks)]

    pairs = GROUP // 2
    together(over(project, keys, w_key, 0))
    together(over(score, 0))
    for pair in range(pairs):
        even, odd = 2 * pair, 2 * pair + 1
        together(over(project, values, w_value, pair), over(raise_, even))
        together(over(score, odd))
        mix(even)
        if pair + 1 < pairs:
            together(over(project, keys, w_key, pair + 1), over(raise_, odd))
            together(over(score, even + 2))
        else:
            together(over(raise_, odd))
        mix(odd)


def attend(lengths, place, material, q_nope, q_rope, w_key, w_value, state, first_back, last):
    tok, wide = q_nope.shape
    heads = wide // HEAD_DIM
    rope = q_rope.shape[1] // heads
    blocks, parts = material[0].shape[0], len(material)
    span, columns = blocks * tok, GROUP * HEAD_DIM
    whole = lambda x: pl.BlockSpec(x.shape, lambda g: (0,) * x.ndim)
    by_group = lambda rows, cols: pl.BlockSpec((rows, cols), lambda g: (0, g))
    stat = pl.BlockSpec((1, tok, 128), lambda g: (g, 0, 0))
    in_specs = [pl.BlockSpec(memory_space=pltpu.SMEM)] * 2
    in_specs += [whole(m) for m in material]
    in_specs += [by_group(tok, columns), by_group(tok, GROUP * rope)]
    in_specs += [by_group(w_key.shape[0], columns)] * 2
    if state:
        in_specs += [by_group(tok, columns), stat]
    if last:
        out_specs = by_group(tok, columns)
        out_shape = jax.ShapeDtypeStruct((tok, wide), bf16)
    else:
        out_specs = [by_group(tok, columns), stat]
        out_shape = [
            jax.ShapeDtypeStruct((tok, wide), f32),
            jax.ShapeDtypeStruct((heads // GROUP, tok, 128), f32),
        ]
    flops = 2 * span * heads * HEAD_DIM * (2 * w_key.shape[0] + 4 * tok)
    return pl.pallas_call(
        functools.partial(
            attend_kernel, (blocks, parts, first_back, not state, last, rope)
        ),
        grid=(heads // GROUP,),
        in_specs=in_specs,
        out_specs=out_specs,
        out_shape=out_shape,
        scratch_shapes=[
            pltpu.VMEM((span, columns), bf16),
            pltpu.VMEM((span, columns), bf16),
            pltpu.VMEM((2, span, 128), bf16),
            pltpu.VMEM((tok, 128), bf16),
            pltpu.VMEM((tok, span), f32),
            pltpu.VMEM((tok, span), f32),
            pltpu.VMEM((tok, span), bf16),
            pltpu.VMEM((tok, span), bf16),
        ],
        compiler_params=pltpu.CompilerParams(vmem_limit_bytes=40 << 20),
        cost_estimate=pl.CostEstimate(
            flops=flops, bytes_accessed=16 << 20, transcendentals=tok * span * heads
        ),
    )(lengths, place, *material, q_nope, q_rope, w_key, w_value, *state)


def shards(q_nope, q_rope, latents, rope_keys, doc_lengths, w_key, w_value):
    head_size = lax.axis_size("head")
    if head_size == 2:
        other_core = lambda x: [x, lax.ppermute(x, "head", [(0, 1), (1, 0)])]
        shift = lax.axis_index("head")
    else:
        latents = lax.all_gather(latents, "head", axis=0, tiled=True)
        rope_keys = lax.all_gather(rope_keys, "head", axis=1, tiled=True)
        other_core = lambda x: [x]
        shift = 0
    place = jnp.stack([lax.axis_index("ctx"), jnp.int32(shift)]).astype(jnp.int32)
    own = pack(latents, rope_keys)
    steps = (q_nope, q_rope, w_key, w_value)
    near = jnp.stack([from_behind(own, by) for by in (1, 2, 3)])
    far = from_behind(jnp.concatenate([own[None], near]), 4)
    state = attend(doc_lengths, place, other_core(own[None]), *steps, (), 0, False)
    state = attend(doc_lengths, place, other_core(near), *steps, state, 1, False)
    return attend(doc_lengths, place, other_core(far), *steps, state, 4, True)


def solution(mesh):
    return jax.shard_map(
        shards,
        mesh=mesh,
        in_specs=(
            P("ctx", "head"),
            P("ctx", "head"),
            P(("ctx", "head"), None),
            P(None, ("ctx", "head")),
            P(),
            P(None, "head"),
            P(None, "head"),
        ),
        out_specs=P("ctx", "head"),
        check_vma=False,
    )
```

```python
import functools
import math

import jax
import jax.numpy as jnp
from jax import lax
from jax.experimental import pallas as pl
from jax.experimental.pallas import tpu as pltpu
from jax.sharding import PartitionSpec as P

HEAD_DIM = 128
WINDOW = 8

masked_score = -1e30
f32, bf16 = jnp.float32, jnp.bfloat16
NT = (((1,), (1,)), ((), ()))


def from_behind(x, by):
    length = lax.axis_size("ctx")
    return lax.ppermute(x, "ctx", [(i, (i + by) % length) for i in range(length)])


def pack_kernel(latents, rope_keys, packed):
    rows = latents.shape[0]
    packed[:rows, :] = latents[...]
    lanes = rope_keys.shape[1]
    pieces = latents.shape[1] // lanes
    tall = rope_keys.shape[0] // pieces
    for piece in range(pieces):
        packed[rows:, piece * lanes : (piece + 1) * lanes] = rope_keys[
            piece * tall : (piece + 1) * tall, :
        ]


def pack(latents, rope_keys):
    rows, width = latents.shape
    below = rope_keys.size // width
    return pl.pallas_call(
        pack_kernel, out_shape=jax.ShapeDtypeStruct((rows + below, width), bf16)
    )(latents, rope_keys)


def weave(*lists):
    calls = [((at + 0.5) / len(each), turn, call) for turn, each in enumerate(lists) for at, call in enumerate(each)]
    for _, _, call in sorted(calls, key=lambda entry: entry[:2]):
        call()


def attend_kernel(shape, *refs):
    blocks, parts, first_back, first, last = shape
    lengths, place = refs[:2]
    material = refs[2 : 2 + parts]
    rest = list(refs[2 + parts :])
    take = lambda count: [rest.pop(0) for _ in range(count)]
    sources = take(4 if first else 6)
    targets = take(1 if last else 2)
    landed = take(len(sources))
    leaving = take(len(targets))
    keys, values, scores_of, weights_of, tops, fades, side, query_side, later, came, went = take(11)
    w_key, q_nope, q_rope, w_value = landed[:4]
    tok = q_nope.shape[1]
    groups = q_nope.shape[0]
    span = blocks * tok
    part_rows = tok // parts
    width = w_key.shape[1]
    rope = q_rope.shape[2] // 4
    scale = math.log2(math.e) / math.sqrt(HEAD_DIM + rope)
    lane = lax.broadcasted_iota(jnp.int32, (tok, 128), 1)
    low = lane < 64

    def columns_of(ref, group, wide):
        if len(ref.shape) == 3:
            return ref.at[group]
        start = group * wide
        return ref.at[:, pl.ds(start if isinstance(start, int) else pl.multiple_of(start, wide), wide)]

    def arrival(which, group):
        into = landed[which].at[group]
        return pltpu.make_async_copy(
            columns_of(sources[which], group, into.shape[-1]), into, came.at[which, group]
        )

    def departure(which, group):
        from_ = leaving[which].at[group]
        return pltpu.make_async_copy(
            from_, columns_of(targets[which], group, from_.shape[-1]), went.at[which, group]
        )

    for group in range(groups):
        for which in range(len(sources)):
            arrival(which, group).start()

    def depart(group):
        for which in range(len(targets)):
            departure(which, group).start()

    at = lax.broadcasted_iota(jnp.int32, (8, 128), 1) % 64
    start, stop = jnp.zeros((8, 128), jnp.int32), jnp.zeros((8, 128), jnp.int32)
    before = jnp.int32(0)
    for doc in range(lengths.shape[0]):
        after = before + lengths[doc]
        start = jnp.where(at == doc, before, start)
        stop = jnp.where(at == doc, after, stop)
        before = after
    start, stop = start[:1], stop[:1]
    row = lax.broadcasted_iota(jnp.int32, (tok, 128), 0)
    position = place[0] * tok + row
    inside = (position >= start) & (position < stop)
    query_side[...] = jnp.where(inside, 1.0, 0.0).astype(bf16)

    def turned(at):
        at = at + place[1] * part_rows
        return jnp.where(at >= tok, at - tok, at)

    if first_back == 0:
        query_at = lax.broadcasted_iota(jnp.int32, (tok, tok), 0)
        key_at = turned(lax.broadcasted_iota(jnp.int32, (tok, tok), 1))
        later[...] = jnp.where(key_at <= query_at, 0.0, masked_score)
    for block in range(blocks):
        position = (place[0] - first_back - block) * tok + turned(row)
        inside = (position >= start) & (position < stop)
        other = jnp.where(inside, 0.0, masked_score)
        rotary = []
        for part in range(parts):
            folded = material[part][block, part_rows:, :].astype(f32)
            pieces = width // part_rows
            flat = jnp.concatenate(
                [folded[:, p * part_rows : (p + 1) * part_rows] for p in range(pieces)], axis=0
            )
            flat = jnp.concatenate([flat, flat], axis=0)
            rotary.append(flat.T)
        rotary = jnp.concatenate(rotary, axis=0)
        rows = slice(block * tok, (block + 1) * tok)
        side[0, rows, :] = jnp.where(low, rotary, other).astype(bf16)
        side[1, rows, :] = jnp.where(low, other, rotary).astype(bf16)

    def latents(block):
        return jnp.concatenate([m[block, :part_rows, :] for m in material], axis=0)

    def project(into, weight, pair, block):
        group, half = pair
        rows = slice(block * tok, (block + 1) * tok)
        columns = slice(half * 256, (half + 1) * 256)
        into[half, rows, :] = jnp.dot(
            latents(block), weight[group, :, columns], preferred_element_type=f32
        ).astype(bf16)

    queries = {}

    def score(pair, odd, block):
        group, half = pair
        rows = slice(block * tok, (block + 1) * tok)
        columns = slice(odd * HEAD_DIM, (odd + 1) * HEAD_DIM)
        head = slice((2 * half + odd) * HEAD_DIM, (2 * half + odd + 1) * HEAD_DIM)
        if block == 0:
            rotary = q_rope[group, :, half * 128 : (half + 1) * 128]
            queries[0] = jnp.concatenate(
                [q_nope[group, :, head], jnp.where(low != (odd == 1), rotary, query_side[...])], axis=1
            )
        key = jnp.concatenate([keys[half, rows, columns], side[odd, rows, :]], axis=1)
        scores = lax.dot_general(queries[0], key, NT, preferred_element_type=f32)
        if first_back + block == 0:
            scores = scores + later[...]
        scores_of[half, odd, :, rows] = scores
        top = jnp.maximum(scores[:, :128], scores[:, 128:])
        queries["top"] = top if block == 0 else jnp.maximum(queries["top"], top)
        if block == blocks - 1:
            top = jnp.max(queries["top"], axis=1, keepdims=True) * scale
            if not first:
                lane_at = 4 * half + odd
                earlier = landed[5][group, :, lane_at : lane_at + 1]
                top = jnp.maximum(top, earlier)
                fades[half, odd] = jnp.broadcast_to(jnp.exp2(earlier - top), (tok, 128))
            tops[half, odd] = jnp.broadcast_to(top, (tok, 128))

    def raise_(pair, odd, block):
        group, half = pair
        rows = slice(block * tok, (block + 1) * tok)
        top = jnp.concatenate([tops[half, odd]] * (tok // 128), axis=1)
        raised = jnp.exp2(scores_of[half, odd, :, rows] * scale - top)
        weights_of[half, odd, :, rows] = raised.astype(bf16)

    def mix(pair, odd):
        group, half = pair
        columns = slice(odd * HEAD_DIM, (odd + 1) * HEAD_DIM)
        head = slice((2 * half + odd) * HEAD_DIM, (2 * half + odd + 1) * HEAD_DIM)
        value = jnp.concatenate([values[half, :, columns], jnp.ones((span, 128), bf16)], axis=1)
        mixed = jnp.dot(weights_of[half, odd], value, preferred_element_type=f32)
        mixed, denom = mixed[:, :128], mixed[:, 128:]
        if not first:
            fade = fades[half, odd]
            mixed = mixed + landed[4][group, :, head] * fade
            lane_at = 4 * half + 2 + odd
            denom = denom + landed[5][group, :, lane_at : lane_at + 1] * fade
        if last:
            mixed = mixed / denom
        else:
            stat = leaving[1][group]
            stat = jnp.where(lane == 4 * half + odd, tops[half, odd], stat)
            leaving[1][group] = jnp.where(lane == 4 * half + 2 + odd, denom, stat)
        leaving[0][group, :, head] = mixed.astype(leaving[0].dtype)

    def each_block(call, *args):
        return [functools.partial(call, *args, block) for block in range(blocks)]

    def both_heads(call, pair):
        return each_block(call, pair, 0) + each_block(call, pair, 1)

    def turn(mixed, scored, keyed):
        raises = both_heads(raise_, mixed)
        half = len(raises) // 2 if keyed else len(raises)
        if scored:
            weave(both_heads(score, scored), raises[:half])
        else:
            weave(raises[:half])
        if keyed:
            weave(each_block(project, keys, w_key, keyed), raises[half:])
        mix(mixed, 0)
        mix(mixed, 1)
        if scored:
            weave(each_block(project, values, w_value, scored))

    arrival(0, 0).wait()
    weave(each_block(project, keys, w_key, (0, 0)))
    for which in range(1, len(sources)):
        arrival(which, 0).wait()
    weave(both_heads(score, (0, 0)), each_block(project, keys, w_key, (0, 1)))
    weave(each_block(project, values, w_value, (0, 0)))

    def two_turns(group, carry):
        for which in range(len(sources)):
            arrival(which, group + 1).wait()

        @pl.when(group > 0)
        def _():
            depart(group - 1)

        turn((group, 0), (group, 1), (group + 1, 0))
        turn((group, 1), (group + 1, 0), (group + 1, 1))
        return carry

    lax.fori_loop(0, groups - 1, two_turns, 0)
    if groups > 1:
        depart(groups - 2)
    turn((groups - 1, 0), (groups - 1, 1), None)
    turn((groups - 1, 1), None, None)
    depart(groups - 1)
    for group in range(groups):
        for which in range(len(targets)):
            departure(which, group).wait()


def attend(lengths, place, material, q_nope, q_rope, w_key, w_value, state, first_back, last):
    tok, wide = q_nope.shape
    groups = wide // HEAD_DIM // 4
    width = w_key.shape[0]
    blocks, parts = material[0].shape[0], len(material)
    span = blocks * tok
    any_ = pl.BlockSpec(memory_space=pl.ANY)
    sources = [w_key, q_nope, q_rope, w_value, *state]
    if last:
        out_shape = [jax.ShapeDtypeStruct((tok, wide), bf16)]
    else:
        out_shape = [
            jax.ShapeDtypeStruct((tok, wide), f32),
            jax.ShapeDtypeStruct((groups, tok, 128), f32),
        ]
    by_pair = lambda x: pltpu.VMEM(
        (groups, x.shape[-2], x.shape[-1] // (groups if len(x.shape) == 2 else 1)), x.dtype
    )
    flops = 2 * span * wide * (2 * width + 4 * tok)
    return pl.pallas_call(
        functools.partial(attend_kernel, (blocks, parts, first_back, not state, last)),
        in_specs=[pl.BlockSpec(memory_space=pltpu.SMEM)] * 2
        + [pl.BlockSpec(memory_space=pltpu.VMEM)] * parts
        + [any_] * len(sources),
        out_specs=[any_] * len(out_shape),
        out_shape=out_shape,
        scratch_shapes=[by_pair(x) for x in sources + out_shape]
        + [
            pltpu.VMEM((2, span, 256), bf16),
            pltpu.VMEM((2, span, 256), bf16),
            pltpu.VMEM((2, 2, tok, span), f32),
            pltpu.VMEM((2, 2, tok, span), bf16),
            pltpu.VMEM((2, 2, tok, 128), f32),
            pltpu.VMEM((2, 2, tok, 128), f32),
            pltpu.VMEM((2, span, 128), bf16),
            pltpu.VMEM((tok, 128), bf16),
            pltpu.VMEM((tok, tok), f32),
            pltpu.SemaphoreType.DMA((len(sources), groups)),
            pltpu.SemaphoreType.DMA((len(out_shape), groups)),
        ],
        compiler_params=pltpu.CompilerParams(vmem_limit_bytes=60 << 20),
        cost_estimate=pl.CostEstimate(
            flops=flops, bytes_accessed=16 << 20, transcendentals=tok * span * wide // HEAD_DIM
        ),
    )(lengths, place, *material, *sources)


def shards(q_nope, q_rope, latents, rope_keys, doc_lengths, w_key, w_value):
    head_size = lax.axis_size("head")
    if head_size == 2:
        other_core = lambda x: [x, lax.ppermute(x, "head", [(0, 1), (1, 0)])]
        shift = lax.axis_index("head")
    else:
        latents = lax.all_gather(latents, "head", axis=0, tiled=True)
        rope_keys = lax.all_gather(rope_keys, "head", axis=1, tiled=True)
        other_core = lambda x: [x]
        shift = 0
    place = jnp.stack([lax.axis_index("ctx"), jnp.int32(shift)]).astype(jnp.int32)
    own = pack(latents, rope_keys)
    steps = (q_nope, q_rope, w_key, w_value)
    near = jnp.stack([from_behind(own, by) for by in (1, 2, 3)])
    far = from_behind(jnp.concatenate([own[None], near]), 4)
    state = attend(doc_lengths, place, other_core(own[None]), *steps, (), 0, False)
    state = attend(doc_lengths, place, other_core(near), *steps, state, 1, False)
    return attend(doc_lengths, place, other_core(far), *steps, state, 4, True)[0]


def solution(mesh):
    return jax.shard_map(
        shards,
        mesh=mesh,
        in_specs=(
            P("ctx", "head"),
            P("ctx", "head"),
            P(("ctx", "head"), None),
            P(None, ("ctx", "head")),
            P(),
            P(None, "head"),
            P(None, "head"),
        ),
        out_specs=P("ctx", "head"),
        check_vma=False,
    )
```

```python
import functools
import math

import jax
import jax.numpy as jnp
from jax import lax
from jax.experimental import pallas as pl
from jax.experimental.pallas import tpu as pltpu
from jax.sharding import PartitionSpec as P

HEAD_DIM = 128
WINDOW = 8

masked_score = -1e30
f32, bf16 = jnp.float32, jnp.bfloat16
NT = (((1,), (1,)), ((), ()))


def from_behind(x, by):
    length = lax.axis_size("ctx")
    return lax.ppermute(x, "ctx", [(i, (i + by) % length) for i in range(length)])


def pack_kernel(latents, rope_keys, packed):
    rows = latents.shape[0]
    packed[:rows, :] = latents[...]
    lanes = rope_keys.shape[1]
    pieces = latents.shape[1] // lanes
    tall = rope_keys.shape[0] // pieces
    for piece in range(pieces):
        packed[rows:, piece * lanes : (piece + 1) * lanes] = rope_keys[
            piece * tall : (piece + 1) * tall, :
        ]


def pack(latents, rope_keys):
    rows, width = latents.shape
    below = rope_keys.size // width
    return pl.pallas_call(
        pack_kernel, out_shape=jax.ShapeDtypeStruct((rows + below, width), bf16)
    )(latents, rope_keys)


def weave(*lists):
    calls = [((at + 0.5) / len(each), turn, call) for turn, each in enumerate(lists) for at, call in enumerate(each)]
    for _, _, call in sorted(calls, key=lambda entry: entry[:2]):
        call()


def attend_kernel(shape, *refs):
    pieces, arrays, diagonal, first, last = shape
    lengths, place = refs[:2]
    rest = list(refs[2:])
    take = lambda count: [rest.pop(0) for _ in range(count)]
    packed = take(arrays)
    sources = take(4 if first else 6)
    targets = take(1 if last else 2)
    material = take(arrays)
    landed = take(len(sources))
    leaving = take(len(targets))
    keys, values, scores_of, weights_of, tops, fades, side, query_side, later, unpacked, came, went = take(12)
    w_key, q_nope, q_rope, w_value = landed[:4]
    tok = q_nope.shape[1]
    groups = q_nope.shape[0]
    part_rows = part_rows_of(packed[0].shape, w_key.shape[1], q_rope.shape[2] // 4)
    span = len(pieces) * part_rows
    bounds = [(at, min(at + tok, span)) for at in range(0, span, tok)]
    blocks = len(bounds)
    width = w_key.shape[1]
    rope = q_rope.shape[2] // 4
    scale = math.log2(math.e) / math.sqrt(HEAD_DIM + rope)
    lane = lax.broadcasted_iota(jnp.int32, (tok, 128), 1)
    low = lane < 64

    def columns_of(ref, group, wide):
        if len(ref.shape) == 3:
            return ref.at[group]
        start = group * wide
        return ref.at[:, pl.ds(start if isinstance(start, int) else pl.multiple_of(start, wide), wide)]

    def arrival(which, group):
        into = landed[which].at[group]
        return pltpu.make_async_copy(
            columns_of(sources[which], group, into.shape[-1]), into, came.at[which, group]
        )

    def departure(which, group):
        from_ = leaving[which].at[group]
        return pltpu.make_async_copy(
            from_, columns_of(targets[which], group, from_.shape[-1]), went.at[which, group]
        )

    arrivals = [
        pltpu.make_async_copy(from_, into, unpacked.at[at])
        for at, (from_, into) in enumerate(zip(packed, material))
    ]
    arrival(0, 0).start()
    for each in arrivals:
        each.start()
    for group in range(groups):
        for which in range(len(sources)):
            if (which, group) != (0, 0):
                arrival(which, group).start()

    def depart(group):
        for which in range(len(targets)):
            departure(which, group).start()

    at = lax.broadcasted_iota(jnp.int32, (8, 128), 1) % 64
    start, stop = jnp.zeros((8, 128), jnp.int32), jnp.zeros((8, 128), jnp.int32)
    before = jnp.int32(0)
    for doc in range(lengths.shape[0]):
        after = before + lengths[doc]
        start = jnp.where(at == doc, before, start)
        stop = jnp.where(at == doc, after, stop)
        before = after
    start, stop = start[:1], stop[:1]
    row = lax.broadcasted_iota(jnp.int32, (tok, 128), 0)
    position = place[0] * tok + row
    inside = (position >= start) & (position < stop)
    query_side[...] = jnp.where(inside, 1.0, 0.0).astype(bf16)

    def turned(at):
        at = at + place[1] * part_rows
        return jnp.where(at >= tok, at - tok, at)

    if diagonal:
        query_at = lax.broadcasted_iota(jnp.int32, (tok, tok), 0)
        key_at = turned(lax.broadcasted_iota(jnp.int32, (tok, tok), 1))
        later[...] = jnp.where(key_at <= query_at, 0.0, masked_score)
    for each in arrivals:
        each.wait()
    folds = width // part_rows
    row = lax.broadcasted_iota(jnp.int32, (part_rows, 128), 0)
    low_rows = lax.broadcasted_iota(jnp.int32, (part_rows, 128), 1) < 64
    for at, (array, index, distance, other) in enumerate(pieces):
        part = 1 - place[1] if other else place[1]
        position = (place[0] - distance) * tok + part * part_rows + row
        inside = (position >= start) & (position < stop)
        elsewhere = jnp.where(inside, 0.0, masked_score)
        folded = material[array][index, part_rows:, :].astype(f32)
        flat = jnp.concatenate(
            [folded[:, p * part_rows : (p + 1) * part_rows] for p in range(folds)] * 2, axis=0
        )
        rotary = flat.T
        rows = slice(at * part_rows, (at + 1) * part_rows)
        side[0, rows, :] = jnp.where(low_rows, rotary, elsewhere).astype(bf16)
        side[1, rows, :] = jnp.where(low_rows, elsewhere, rotary).astype(bf16)

    def latents(block):
        low_end, high_end = (bound // part_rows for bound in bounds[block])
        return jnp.concatenate(
            [material[array][index, :part_rows, :] for array, index, _, _ in pieces[low_end:high_end]],
            axis=0,
        )

    def project(into, weight, pair, block):
        group, half = pair
        rows = slice(*bounds[block])
        columns = slice(half * 256, (half + 1) * 256)
        into[half, rows, :] = jnp.dot(
            latents(block), weight[group, :, columns], preferred_element_type=f32
        ).astype(bf16)

    queries = {}

    def score(pair, odd, block):
        group, half = pair
        rows = slice(*bounds[block])
        columns = slice(odd * HEAD_DIM, (odd + 1) * HEAD_DIM)
        head = slice((2 * half + odd) * HEAD_DIM, (2 * half + odd + 1) * HEAD_DIM)
        if block == 0:
            rotary = q_rope[group, :, half * 128 : (half + 1) * 128]
            queries[0] = jnp.concatenate(
                [q_nope[group, :, head], jnp.where(low != (odd == 1), rotary, query_side[...])], axis=1
            )
        key = jnp.concatenate([keys[half, rows, columns], side[odd, rows, :]], axis=1)
        scores = lax.dot_general(queries[0], key, NT, preferred_element_type=f32)
        if diagonal and block == 0:
            scores = scores + later[...]
        scores_of[half, odd, :, rows] = scores
        top = functools.reduce(
            jnp.maximum, [scores[:, at : at + 128] for at in range(0, scores.shape[1], 128)]
        )
        queries["top"] = top if block == 0 else jnp.maximum(queries["top"], top)
        if block == blocks - 1:
            top = jnp.max(queries["top"], axis=1, keepdims=True) * scale
            if not first:
                lane_at = 4 * half + odd
                earlier = landed[5][group, :, lane_at : lane_at + 1]
                top = jnp.maximum(top, earlier)
                fades[half, odd] = jnp.broadcast_to(jnp.exp2(earlier - top), (tok, 128))
            tops[half, odd] = jnp.broadcast_to(top, (tok, 128))

    def raise_(pair, odd, block):
        group, half = pair
        rows = slice(*bounds[block])
        top = jnp.concatenate([tops[half, odd]] * ((rows.stop - rows.start) // 128), axis=1)
        raised = jnp.exp2(scores_of[half, odd, :, rows] * scale - top)
        weights_of[half, odd, :, rows] = raised.astype(bf16)

    def mix(pair, odd):
        group, half = pair
        columns = slice(odd * HEAD_DIM, (odd + 1) * HEAD_DIM)
        head = slice((2 * half + odd) * HEAD_DIM, (2 * half + odd + 1) * HEAD_DIM)
        value = jnp.concatenate([values[half, :, columns], jnp.ones((span, 128), bf16)], axis=1)
        mixed = jnp.dot(weights_of[half, odd], value, preferred_element_type=f32)
        mixed, denom = mixed[:, :128], mixed[:, 128:]
        if not first:
            fade = fades[half, odd]
            mixed = mixed + landed[4][group, :, head] * fade
            lane_at = 4 * half + 2 + odd
            denom = denom + landed[5][group, :, lane_at : lane_at + 1] * fade
        if last:
            mixed = mixed / denom
        else:
            stat = leaving[1][group]
            stat = jnp.where(lane == 4 * half + odd, tops[half, odd], stat)
            leaving[1][group] = jnp.where(lane == 4 * half + 2 + odd, denom, stat)
        leaving[0][group, :, head] = mixed.astype(leaving[0].dtype)

    def each_block(call, *args):
        return [functools.partial(call, *args, block) for block in range(blocks)]

    def both_heads(call, pair):
        return each_block(call, pair, 0) + each_block(call, pair, 1)

    def turn(mixed, scored, keyed):
        raises = both_heads(raise_, mixed)
        half = len(raises) // 2 if keyed else len(raises)
        if scored:
            weave(both_heads(score, scored), raises[:half])
        else:
            weave(raises[:half])
        if keyed:
            weave(each_block(project, keys, w_key, keyed), raises[half:])
        mix(mixed, 0)
        mix(mixed, 1)
        if scored:
            weave(each_block(project, values, w_value, scored))

    arrival(0, 0).wait()
    weave(each_block(project, keys, w_key, (0, 0)))
    for which in range(1, len(sources)):
        arrival(which, 0).wait()
    weave(both_heads(score, (0, 0)), each_block(project, keys, w_key, (0, 1)))
    weave(each_block(project, values, w_value, (0, 0)))

    def two_turns(group, carry):
        for which in range(len(sources)):
            arrival(which, group + 1).wait()

        @pl.when(group > 0)
        def _():
            depart(group - 1)

        turn((group, 0), (group, 1), (group + 1, 0))
        turn((group, 1), (group + 1, 0), (group + 1, 1))
        return carry

    lax.fori_loop(0, groups - 1, two_turns, 0)
    if groups > 1:
        depart(groups - 2)
    turn((groups - 1, 0), (groups - 1, 1), None)
    turn((groups - 1, 1), None, None)
    depart(groups - 1)
    for group in range(groups):
        for which in range(len(targets)):
            departure(which, group).wait()


def part_rows_of(packed_shape, width, rope):
    return packed_shape[1] * width // (width + rope)


def attend(lengths, place, material, pieces, q_nope, q_rope, w_key, w_value, state, diagonal, last):
    tok, wide = q_nope.shape
    groups = wide // HEAD_DIM // 4
    width = w_key.shape[0]
    rope = q_rope.shape[1] * HEAD_DIM // wide
    span = len(pieces) * part_rows_of(material[0].shape, width, rope)
    any_ = pl.BlockSpec(memory_space=pl.ANY)
    sources = [w_key, q_nope, q_rope, w_value, *state]
    if last:
        out_shape = [jax.ShapeDtypeStruct((tok, wide), bf16)]
    else:
        out_shape = [
            jax.ShapeDtypeStruct((tok, wide), f32),
            jax.ShapeDtypeStruct((groups, tok, 128), f32),
        ]
    by_group = lambda x: pltpu.VMEM(
        (groups, x.shape[-2], x.shape[-1] // (groups if len(x.shape) == 2 else 1)), x.dtype
    )
    flops = 2 * span * wide * (2 * width + 4 * tok)
    return pl.pallas_call(
        functools.partial(attend_kernel, (pieces, len(material), diagonal, not state, last)),
        in_specs=[pl.BlockSpec(memory_space=pltpu.SMEM)] * 2
        + [any_] * (len(material) + len(sources)),
        out_specs=[any_] * len(out_shape),
        out_shape=out_shape,
        scratch_shapes=[pltpu.VMEM(x.shape, x.dtype) for x in material]
        + [by_group(x) for x in sources + out_shape]
        + [
            pltpu.VMEM((2, span, 256), bf16),
            pltpu.VMEM((2, span, 256), bf16),
            pltpu.VMEM((2, 2, tok, span), f32),
            pltpu.VMEM((2, 2, tok, span), bf16),
            pltpu.VMEM((2, 2, tok, 128), f32),
            pltpu.VMEM((2, 2, tok, 128), f32),
            pltpu.VMEM((2, span, 128), bf16),
            pltpu.VMEM((tok, 128), bf16),
            pltpu.VMEM((tok, tok), f32),
            pltpu.SemaphoreType.DMA((len(material),)),
            pltpu.SemaphoreType.DMA((len(sources), groups)),
            pltpu.SemaphoreType.DMA((len(out_shape), groups)),
        ],
        compiler_params=pltpu.CompilerParams(vmem_limit_bytes=60 << 20),
        cost_estimate=pl.CostEstimate(
            flops=flops, bytes_accessed=16 << 20, transcendentals=tok * span * wide // HEAD_DIM
        ),
    )(lengths, place, *material, *sources)


def shards(q_nope, q_rope, latents, rope_keys, doc_lengths, w_key, w_value):
    halves = lax.axis_size("head") == 2
    place = [lax.axis_index("ctx"), lax.axis_index("head") if halves else jnp.int32(0)]
    place = jnp.stack(place).astype(jnp.int32)
    if halves:
        swap = lambda x: lax.ppermute(x, "head", [(0, 1), (1, 0)])
    else:
        latents = lax.all_gather(latents, "head", axis=0, tiled=True)
        rope_keys = lax.all_gather(rope_keys, "head", axis=1, tiled=True)
    run = lambda material, pieces, state, last: attend(
        doc_lengths, place, material, pieces, q_nope, q_rope, w_key, w_value, state, not state, last
    )
    own = pack(latents, rope_keys)
    near = [from_behind(own, by) for by in (1, 2, 3)]
    if halves:
        state = run([own[None], swap(own[None])], [(0, 0, 0, False), (1, 0, 0, True)], (), False)
    else:
        state = run([own[None]], [(0, 0, 0, False)], (), False)
    near, state = lax.optimization_barrier((near, state))
    near = jnp.stack(near)
    far = from_behind(jnp.concatenate([own[None], near]), 4)
    near_pieces = [(0, block - 1, block, False) for block in (1, 2, 3)]
    far_pieces = [(0, block - 4, block, False) for block in (4, 5, 6, 7)]
    if halves:
        other_near = swap(near)
        state = run([near], near_pieces, state, False)
        far_pieces += [(1, block - 4, block, True) for block in (4, 5, 6, 7)]
        far_pieces += [(2, block - 1, block, True) for block in (1, 2, 3)]
        return run([far, swap(far), other_near], far_pieces, state, True)[0]
    state = run([near], near_pieces, state, False)
    return run([far], far_pieces, state, True)[0]


def solution(mesh):
    return jax.shard_map(
        shards,
        mesh=mesh,
        in_specs=(
            P("ctx", "head"),
            P("ctx", "head"),
            P(("ctx", "head"), None),
            P(None, ("ctx", "head")),
            P(),
            P(None, "head"),
            P(None, "head"),
        ),
        out_specs=P("ctx", "head"),
        check_vma=False,
    )
```

```python
import functools
import math

import jax
import jax.numpy as jnp
from jax import lax
from jax.experimental import pallas as pl
from jax.experimental.pallas import tpu as pltpu
from jax.sharding import PartitionSpec as P

HEAD_DIM = 128
WINDOW = 8

masked_score = -1e30
f32, bf16 = jnp.float32, jnp.bfloat16
NT = (((1,), (1,)), ((), ()))


def from_behind(x, by):
    length = lax.axis_size("ctx")
    return lax.ppermute(x, "ctx", [(i, (i + by) % length) for i in range(length)])


def pack_kernel(latents, rope_keys, packed):
    rows = latents.shape[0]
    packed[:rows, :] = latents[...]
    lanes = rope_keys.shape[1]
    pieces = latents.shape[1] // lanes
    tall = rope_keys.shape[0] // pieces
    for piece in range(pieces):
        packed[rows:, piece * lanes : (piece + 1) * lanes] = rope_keys[
            piece * tall : (piece + 1) * tall, :
        ]


def pack(latents, rope_keys):
    rows, width = latents.shape
    below = rope_keys.size // width
    return pl.pallas_call(
        pack_kernel, out_shape=jax.ShapeDtypeStruct((rows + below, width), bf16)
    )(latents, rope_keys)


def weave(*lists):
    calls = [((at + 0.5) / len(each), turn, call) for turn, each in enumerate(lists) for at, call in enumerate(each)]
    for _, _, call in sorted(calls, key=lambda entry: entry[:2]):
        call()


def attend_kernel(shape, *refs):
    pieces, arrays, diagonal, first, last = shape
    lengths, place = refs[:2]
    rest = list(refs[2:])
    take = lambda count: [rest.pop(0) for _ in range(count)]
    packed = take(arrays)
    sources = take(4 if first else 6)
    targets = take(1 if last else 2)
    material = packed
    landed = take(len(sources))
    leaving = take(len(targets))
    keys, values, scores_of, weights_of, tops, fades, side, query_side, later, unpacked, came, went = take(12)
    w_key, q_nope, q_rope, w_value = landed[:4]
    tok = q_nope.shape[1]
    groups = q_nope.shape[0]
    part_rows = part_rows_of(packed[0].shape, w_key.shape[1], q_rope.shape[2] // 4)
    span = len(pieces) * part_rows
    bounds = [(at, min(at + tok, span)) for at in range(0, span, tok)]
    blocks = len(bounds)
    width = w_key.shape[1]
    rope = q_rope.shape[2] // 4
    scale = math.log2(math.e) / math.sqrt(HEAD_DIM + rope)
    lane = lax.broadcasted_iota(jnp.int32, (tok, 128), 1)
    low = lane < 64

    def columns_of(ref, group, wide):
        if len(ref.shape) == 3:
            return ref.at[group]
        start = group * wide
        return ref.at[:, pl.ds(start if isinstance(start, int) else pl.multiple_of(start, wide), wide)]

    def arrival(which, group):
        into = landed[which].at[group]
        return pltpu.make_async_copy(
            columns_of(sources[which], group, into.shape[-1]), into, came.at[which, group]
        )

    def departure(which, group):
        from_ = leaving[which].at[group]
        return pltpu.make_async_copy(
            from_, columns_of(targets[which], group, from_.shape[-1]), went.at[which, group]
        )

    for which in range(len(sources)):
        arrival(which, 0).start()
    for group in range(1, groups):
        for which in range(len(sources)):
            arrival(which, group).start()

    def depart(group):
        for which in range(len(targets)):
            departure(which, group).start()

    at = lax.broadcasted_iota(jnp.int32, (8, 128), 1) % 64
    start, stop = jnp.zeros((8, 128), jnp.int32), jnp.zeros((8, 128), jnp.int32)
    before = jnp.int32(0)
    for doc in range(lengths.shape[0]):
        after = before + lengths[doc]
        start = jnp.where(at == doc, before, start)
        stop = jnp.where(at == doc, after, stop)
        before = after
    start, stop = start[:1], stop[:1]
    row = lax.broadcasted_iota(jnp.int32, (tok, 128), 0)
    position = place[0] * tok + row
    inside = (position >= start) & (position < stop)
    query_side[...] = jnp.where(inside, 1.0, 0.0).astype(bf16)

    def turned(at):
        at = at + place[1] * part_rows
        return jnp.where(at >= tok, at - tok, at)

    if diagonal:
        query_at = lax.broadcasted_iota(jnp.int32, (tok, tok), 0)
        key_at = turned(lax.broadcasted_iota(jnp.int32, (tok, tok), 1))
        later[...] = jnp.where(key_at <= query_at, 0.0, masked_score)
    folds = width // part_rows
    row = lax.broadcasted_iota(jnp.int32, (part_rows, 128), 0)
    low_rows = lax.broadcasted_iota(jnp.int32, (part_rows, 128), 1) < 64
    for at, (array, index, distance, other) in enumerate(pieces):
        part = 1 - place[1] if other else place[1]
        position = (place[0] - distance) * tok + part * part_rows + row
        inside = (position >= start) & (position < stop)
        elsewhere = jnp.where(inside, 0.0, masked_score)
        folded = material[array][index, part_rows:, :].astype(f32)
        flat = jnp.concatenate(
            [folded[:, p * part_rows : (p + 1) * part_rows] for p in range(folds)] * 2, axis=0
        )
        rotary = flat.T
        rows = slice(at * part_rows, (at + 1) * part_rows)
        side[0, rows, :] = jnp.where(low_rows, rotary, elsewhere).astype(bf16)
        side[1, rows, :] = jnp.where(low_rows, elsewhere, rotary).astype(bf16)

    def latents(block):
        low_end, high_end = (bound // part_rows for bound in bounds[block])
        return jnp.concatenate(
            [material[array][index, :part_rows, :] for array, index, _, _ in pieces[low_end:high_end]],
            axis=0,
        )

    def project(into, weight, pair, block):
        group, half = pair
        rows = slice(*bounds[block])
        columns = slice(half * 256, (half + 1) * 256)
        into[half, rows, :] = jnp.dot(
            latents(block), weight[group, :, columns], preferred_element_type=f32
        ).astype(bf16)

    queries = {}

    def score(pair, odd, block):
        group, half = pair
        rows = slice(*bounds[block])
        columns = slice(odd * HEAD_DIM, (odd + 1) * HEAD_DIM)
        head = slice((2 * half + odd) * HEAD_DIM, (2 * half + odd + 1) * HEAD_DIM)
        if block == 0:
            rotary = q_rope[group, :, half * 128 : (half + 1) * 128]
            queries[0] = jnp.concatenate(
                [q_nope[group, :, head], jnp.where(low != (odd == 1), rotary, query_side[...])], axis=1
            )
        key = jnp.concatenate([keys[half, rows, columns], side[odd, rows, :]], axis=1)
        scores = lax.dot_general(queries[0], key, NT, preferred_element_type=f32)
        if diagonal and block == 0:
            scores = scores + later[...]
        scores_of[half, odd, :, rows] = scores
        top = functools.reduce(
            jnp.maximum, [scores[:, at : at + 128] for at in range(0, scores.shape[1], 128)]
        )
        queries["top"] = top if block == 0 else jnp.maximum(queries["top"], top)
        if block == blocks - 1:
            top = jnp.max(queries["top"], axis=1, keepdims=True) * scale
            if not first:
                lane_at = 4 * half + odd
                earlier = landed[5][group, :, lane_at : lane_at + 1]
                top = jnp.maximum(top, earlier)
                fades[half, odd] = jnp.broadcast_to(jnp.exp2(earlier - top), (tok, 128))
            tops[half, odd] = jnp.broadcast_to(top, (tok, 128))

    def raise_(pair, odd, block):
        group, half = pair
        rows = slice(*bounds[block])
        top = jnp.concatenate([tops[half, odd]] * ((rows.stop - rows.start) // 128), axis=1)
        raised = jnp.exp2(scores_of[half, odd, :, rows] * scale - top)
        weights_of[half, odd, :, rows] = raised.astype(bf16)

    def mix(pair, odd):
        group, half = pair
        columns = slice(odd * HEAD_DIM, (odd + 1) * HEAD_DIM)
        head = slice((2 * half + odd) * HEAD_DIM, (2 * half + odd + 1) * HEAD_DIM)
        value = jnp.concatenate([values[half, :, columns], jnp.ones((span, 128), bf16)], axis=1)
        mixed = jnp.dot(weights_of[half, odd], value, preferred_element_type=f32)
        mixed, denom = mixed[:, :128], mixed[:, 128:]
        if not first:
            fade = fades[half, odd]
            mixed = mixed + landed[4][group, :, head] * fade
            lane_at = 4 * half + 2 + odd
            denom = denom + landed[5][group, :, lane_at : lane_at + 1] * fade
        if last:
            mixed = mixed / denom
        else:
            stat = leaving[1][group]
            stat = jnp.where(lane == 4 * half + odd, tops[half, odd], stat)
            leaving[1][group] = jnp.where(lane == 4 * half + 2 + odd, denom, stat)
        leaving[0][group, :, head] = mixed.astype(leaving[0].dtype)

    def each_block(call, *args):
        return [functools.partial(call, *args, block) for block in range(blocks)]

    def both_heads(call, pair):
        return each_block(call, pair, 0) + each_block(call, pair, 1)

    def turn(mixed, scored, keyed):
        raises = both_heads(raise_, mixed)
        half = len(raises) // 2 if keyed else len(raises)
        if scored:
            weave(both_heads(score, scored), raises[:half])
        else:
            weave(raises[:half])
        if keyed:
            weave(each_block(project, keys, w_key, keyed), raises[half:])
        mix(mixed, 0)
        mix(mixed, 1)
        if scored:
            weave(each_block(project, values, w_value, scored))

    arrival(0, 0).wait()
    weave(each_block(project, keys, w_key, (0, 0)))
    for which in range(1, len(sources)):
        arrival(which, 0).wait()
    weave(both_heads(score, (0, 0)), each_block(project, keys, w_key, (0, 1)))
    weave(each_block(project, values, w_value, (0, 0)))

    def two_turns(group, carry):
        for which in range(len(sources)):
            arrival(which, group + 1).wait()

        @pl.when(group > 0)
        def _():
            depart(group - 1)

        turn((group, 0), (group, 1), (group + 1, 0))
        turn((group, 1), (group + 1, 0), (group + 1, 1))
        return carry

    lax.fori_loop(0, groups - 1, two_turns, 0)
    if groups > 1:
        depart(groups - 2)
    turn((groups - 1, 0), (groups - 1, 1), None)
    turn((groups - 1, 1), None, None)
    depart(groups - 1)
    for group in range(groups):
        for which in range(len(targets)):
            departure(which, group).wait()


def part_rows_of(packed_shape, width, rope):
    return packed_shape[1] * width // (width + rope)


def attend(lengths, place, material, pieces, q_nope, q_rope, w_key, w_value, state, diagonal, last):
    tok, wide = q_nope.shape
    groups = wide // HEAD_DIM // 4
    width = w_key.shape[0]
    rope = q_rope.shape[1] * HEAD_DIM // wide
    span = len(pieces) * part_rows_of(material[0].shape, width, rope)
    any_ = pl.BlockSpec(memory_space=pl.ANY)
    sources = [w_key, q_nope, q_rope, w_value, *state]
    if last:
        out_shape = [jax.ShapeDtypeStruct((tok, wide), bf16)]
    else:
        out_shape = [
            jax.ShapeDtypeStruct((tok, wide), f32),
            jax.ShapeDtypeStruct((groups, tok, 128), f32),
        ]
    by_group = lambda x: pltpu.VMEM(
        (groups, x.shape[-2], x.shape[-1] // (groups if len(x.shape) == 2 else 1)), x.dtype
    )
    flops = 2 * span * wide * (2 * width + 4 * tok)
    return pl.pallas_call(
        functools.partial(attend_kernel, (pieces, len(material), diagonal, not state, last)),
        in_specs=[pl.BlockSpec(memory_space=pltpu.SMEM)] * 2
        + [pl.BlockSpec(memory_space=pltpu.VMEM)] * len(material) + [any_] * len(sources),
        out_specs=[any_] * len(out_shape),
        out_shape=out_shape,
        scratch_shapes=[by_group(x) for x in sources + out_shape]
        + [
            pltpu.VMEM((2, span, 256), bf16),
            pltpu.VMEM((2, span, 256), bf16),
            pltpu.VMEM((2, 2, tok, span), f32),
            pltpu.VMEM((2, 2, tok, span), bf16),
            pltpu.VMEM((2, 2, tok, 128), f32),
            pltpu.VMEM((2, 2, tok, 128), f32),
            pltpu.VMEM((2, span, 128), bf16),
            pltpu.VMEM((tok, 128), bf16),
            pltpu.VMEM((tok, tok), f32),
            pltpu.SemaphoreType.DMA((len(material),)),
            pltpu.SemaphoreType.DMA((len(sources), groups)),
            pltpu.SemaphoreType.DMA((len(out_shape), groups)),
        ],
        compiler_params=pltpu.CompilerParams(vmem_limit_bytes=60 << 20),
        cost_estimate=pl.CostEstimate(
            flops=flops, bytes_accessed=16 << 20, transcendentals=tok * span * wide // HEAD_DIM
        ),
    )(lengths, place, *material, *sources)


def shards(q_nope, q_rope, latents, rope_keys, doc_lengths, w_key, w_value):
    halves = lax.axis_size("head") == 2
    place = [lax.axis_index("ctx"), lax.axis_index("head") if halves else jnp.int32(0)]
    place = jnp.stack(place).astype(jnp.int32)
    if halves:
        swap = lambda x: lax.ppermute(x, "head", [(0, 1), (1, 0)])
    else:
        latents = lax.all_gather(latents, "head", axis=0, tiled=True)
        rope_keys = lax.all_gather(rope_keys, "head", axis=1, tiled=True)
    run = lambda material, pieces, state, last: attend(
        doc_lengths, place, material, pieces, q_nope, q_rope, w_key, w_value, state, not state, last
    )
    own = pack(latents, rope_keys)
    near = [from_behind(own, by) for by in (1, 2, 3)]
    if halves:
        state = run([own[None], swap(own[None])], [(0, 0, 0, False), (1, 0, 0, True)], (), False)
    else:
        state = run([own[None]], [(0, 0, 0, False)], (), False)
    near, state = lax.optimization_barrier((near, state))
    near = jnp.stack(near)
    far = from_behind(jnp.concatenate([own[None], near]), 4)
    near_pieces = [(0, block - 1, block, False) for block in (1, 2, 3)]
    far_pieces = [(0, block - 4, block, False) for block in (4, 5, 6, 7)]
    if halves:
        near_pieces += [(1, block - 1, block, True) for block in (1, 2, 3)]
        far_pieces += [(1, block - 4, block, True) for block in (4, 5, 6, 7)]
        both = lambda x: [x, swap(x)]
    else:
        both = lambda x: [x]
    state = run(both(near), near_pieces, state, False)
    far, state = lax.optimization_barrier((far, state))
    return run(both(far), far_pieces, state, True)[0]


def solution(mesh):
    return jax.shard_map(
        shards,
        mesh=mesh,
        in_specs=(
            P("ctx", "head"),
            P("ctx", "head"),
            P(("ctx", "head"), None),
            P(None, ("ctx", "head")),
            P(),
            P(None, "head"),
            P(None, "head"),
        ),
        out_specs=P("ctx", "head"),
        check_vma=False,
    )
```

```python
import functools
import math

import jax
import jax.numpy as jnp
from jax import lax
from jax.experimental import pallas as pl
from jax.experimental.pallas import tpu as pltpu
from jax.sharding import PartitionSpec as P

HEAD_DIM = 128
WINDOW = 8

masked_score = -1e30
f32, bf16 = jnp.float32, jnp.bfloat16
NT = (((1,), (1,)), ((), ()))


def from_behind(x, by):
    length = lax.axis_size("ctx")
    return lax.ppermute(x, "ctx", [(i, (i + by) % length) for i in range(length)])


def pack_kernel(latents, rope_keys, packed):
    rows = latents.shape[0]
    packed[:rows, :] = latents[...]
    lanes = rope_keys.shape[1]
    pieces = latents.shape[1] // lanes
    tall = rope_keys.shape[0] // pieces
    for piece in range(pieces):
        packed[rows:, piece * lanes : (piece + 1) * lanes] = rope_keys[
            piece * tall : (piece + 1) * tall, :
        ]


def pack(latents, rope_keys):
    rows, width = latents.shape
    below = rope_keys.size // width
    return pl.pallas_call(
        pack_kernel, out_shape=jax.ShapeDtypeStruct((rows + below, width), bf16)
    )(latents, rope_keys)


def weave(*lists):
    calls = [((at + 0.5) / len(each), turn, call) for turn, each in enumerate(lists) for at, call in enumerate(each)]
    for _, _, call in sorted(calls, key=lambda entry: entry[:2]):
        call()


def attend_kernel(shape, *refs):
    pieces, arrays, halves, diagonal, first, last = shape
    lengths = refs[0]
    rest = list(refs[1:])
    place = (lax.axis_index("ctx"), lax.axis_index("head") if halves else 0)
    take = lambda count: [rest.pop(0) for _ in range(count)]
    packed = take(arrays)
    sources = take(4 if first else 6)
    targets = take(1 if last else 2)
    material = packed
    landed = take(len(sources))
    leaving = take(len(targets))
    keys, values, scores_of, weights_of, tops, fades, side, query_side, later, unpacked, came, went = take(12)
    w_key, q_nope, q_rope, w_value = landed[:4]
    tok = q_nope.shape[1]
    groups = q_nope.shape[0]
    part_rows = part_rows_of(packed[0].shape, w_key.shape[1], q_rope.shape[2] // 4)
    span = len(pieces) * part_rows
    bounds = [(at, min(at + tok, span)) for at in range(0, span, tok)]
    blocks = len(bounds)
    width = w_key.shape[1]
    rope = q_rope.shape[2] // 4
    scale = math.log2(math.e) / math.sqrt(HEAD_DIM + rope)
    lane = lax.broadcasted_iota(jnp.int32, (tok, 128), 1)
    low = lane < 64

    def columns_of(ref, group, wide):
        if len(ref.shape) == 3:
            return ref.at[group]
        start = group * wide
        return ref.at[:, pl.ds(start if isinstance(start, int) else pl.multiple_of(start, wide), wide)]

    def arrival(which, group):
        into = landed[which].at[group]
        return pltpu.make_async_copy(
            columns_of(sources[which], group, into.shape[-1]), into, came.at[which, group]
        )

    def departure(which, group):
        from_ = leaving[which].at[group]
        return pltpu.make_async_copy(
            from_, columns_of(targets[which], group, from_.shape[-1]), went.at[which, group]
        )

    for which in range(len(sources)):
        arrival(which, 0).start()
    for group in range(1, groups):
        for which in range(len(sources)):
            arrival(which, group).start()

    def depart(group):
        for which in range(len(targets)):
            departure(which, group).start()

    at = lax.broadcasted_iota(jnp.int32, (8, 128), 1) % 64
    start, stop = jnp.zeros((8, 128), jnp.int32), jnp.zeros((8, 128), jnp.int32)
    before = jnp.int32(0)
    for doc in range(lengths.shape[0]):
        after = before + lengths[doc]
        start = jnp.where(at == doc, before, start)
        stop = jnp.where(at == doc, after, stop)
        before = after
    start, stop = start[:1], stop[:1]
    row = lax.broadcasted_iota(jnp.int32, (tok, 128), 0)
    position = place[0] * tok + row
    inside = (position >= start) & (position < stop)
    query_side[...] = jnp.where(inside, 1.0, 0.0).astype(bf16)

    def turned(at):
        at = at + place[1] * part_rows
        return jnp.where(at >= tok, at - tok, at)

    if diagonal:
        query_at = lax.broadcasted_iota(jnp.int32, (tok, tok), 0)
        key_at = turned(lax.broadcasted_iota(jnp.int32, (tok, tok), 1))
        later[...] = jnp.where(key_at <= query_at, 0.0, masked_score)
    folds = width // part_rows
    row = lax.broadcasted_iota(jnp.int32, (part_rows, 128), 0)
    low_rows = lax.broadcasted_iota(jnp.int32, (part_rows, 128), 1) < 64
    for at, (array, index, distance, other) in enumerate(pieces):
        part = 1 - place[1] if other else place[1]
        position = (place[0] - distance) * tok + part * part_rows + row
        inside = (position >= start) & (position < stop)
        elsewhere = jnp.where(inside, 0.0, masked_score)
        folded = material[array][index, part_rows:, :].astype(f32)
        flat = jnp.concatenate(
            [folded[:, p * part_rows : (p + 1) * part_rows] for p in range(folds)] * 2, axis=0
        )
        rotary = flat.T
        rows = slice(at * part_rows, (at + 1) * part_rows)
        side[0, rows, :] = jnp.where(low_rows, rotary, elsewhere).astype(bf16)
        side[1, rows, :] = jnp.where(low_rows, elsewhere, rotary).astype(bf16)

    def latents(block):
        low_end, high_end = (bound // part_rows for bound in bounds[block])
        return jnp.concatenate(
            [material[array][index, :part_rows, :] for array, index, _, _ in pieces[low_end:high_end]],
            axis=0,
        )

    def work(tall, blocks):
        reach = bounds[blocks - 1][1]

        def project(into, weight, pair, block):
            group, half = pair
            rows = slice(*bounds[block])
            columns = slice(half * 256, (half + 1) * 256)
            into[half, rows, :] = jnp.dot(
                latents(block), weight[group, :, columns], preferred_element_type=f32
            ).astype(bf16)

        queries = {}

        def score(pair, odd, block):
            group, half = pair
            rows = slice(*bounds[block])
            columns = slice(odd * HEAD_DIM, (odd + 1) * HEAD_DIM)
            head = slice((2 * half + odd) * HEAD_DIM, (2 * half + odd + 1) * HEAD_DIM)
            if block == 0:
                rotary = q_rope[group, :tall, half * 128 : (half + 1) * 128]
                queries[0] = jnp.concatenate(
                    [q_nope[group, :tall, head], jnp.where(low[:tall] != (odd == 1), rotary, query_side[:tall, :])],
                        axis=1,
                )
            key = jnp.concatenate([keys[half, rows, columns], side[odd, rows, :]], axis=1)
            scores = lax.dot_general(queries[0], key, NT, preferred_element_type=f32)
            if diagonal and block == 0:
                scores = scores + later[...]
            scores_of[half, odd, :tall, rows] = scores
            top = functools.reduce(
                jnp.maximum, [scores[:, at : at + 128] for at in range(0, scores.shape[1], 128)]
            )
            queries["top"] = top if block == 0 else jnp.maximum(queries["top"], top)
            if block == blocks - 1:
                top = jnp.max(queries["top"], axis=1, keepdims=True) * scale
                if not first:
                    lane_at = 4 * half + odd
                    earlier = landed[5][group, :tall, lane_at : lane_at + 1]
                    top = jnp.maximum(top, earlier)
                    fades[half, odd, :tall] = jnp.broadcast_to(jnp.exp2(earlier - top), (tall, 128))
                tops[half, odd, :tall] = jnp.broadcast_to(top, (tall, 128))

        def raise_(pair, odd, block):
            group, half = pair
            rows = slice(*bounds[block])
            top = jnp.concatenate([tops[half, odd, :tall]] * ((rows.stop - rows.start) // 128), axis=1)
            raised = jnp.exp2(scores_of[half, odd, :tall, rows] * scale - top)
            weights_of[half, odd, :tall, rows] = raised.astype(bf16)

        def mix(pair, odd):
            group, half = pair
            columns = slice(odd * HEAD_DIM, (odd + 1) * HEAD_DIM)
            head = slice((2 * half + odd) * HEAD_DIM, (2 * half + odd + 1) * HEAD_DIM)
            value = jnp.concatenate(
                [values[half, :reach, columns], jnp.ones((reach, 128), bf16)], axis=1
            )
            mixed = jnp.dot(weights_of[half, odd, :tall, :reach], value, preferred_element_type=f32)
            mixed, denom = mixed[:, :128], mixed[:, 128:]
            if not first:
                fade = fades[half, odd, :tall]
                mixed = mixed + landed[4][group, :tall, head] * fade
                lane_at = 4 * half + 2 + odd
                denom = denom + landed[5][group, :tall, lane_at : lane_at + 1] * fade
            if last:
                mixed = mixed / denom
            else:
                stat = leaving[1][group, :tall]
                stat = jnp.where(lane[:tall] == 4 * half + odd, tops[half, odd, :tall], stat)
                stat = jnp.where(lane[:tall] == 4 * half + 2 + odd, denom, stat)
                leaving[1][group, :tall] = stat
            leaving[0][group, :tall, head] = mixed.astype(leaving[0].dtype)
            if tall < tok:
                others = landed[4][group, tall:, head]
                if last:
                    others = others / landed[5][group, tall:, lane_at : lane_at + 1]
                elif odd == 1:
                    stat = landed[5][group, tall:]
                    pair_lanes = (lane[tall:] >= 4 * half) & (lane[tall:] < 4 * half + 4)
                    leaving[1][group, tall:] = jnp.where(pair_lanes, stat, leaving[1][group, tall:])
                leaving[0][group, tall:, head] = others.astype(leaving[0].dtype)

        def each_block(call, *args):
            return [functools.partial(call, *args, block) for block in range(blocks)]

        def both_heads(call, pair):
            return each_block(call, pair, 0) + each_block(call, pair, 1)

        def turn(mixed, scored, keyed):
            raises = both_heads(raise_, mixed)
            half = len(raises) // 2 if keyed else len(raises)
            if scored:
                weave(both_heads(score, scored), raises[:half])
            else:
                weave(raises[:half])
            if keyed:
                weave(each_block(project, keys, w_key, keyed), raises[half:])
            mix(mixed, 0)
            mix(mixed, 1)
            if scored:
                weave(each_block(project, values, w_value, scored))

        arrival(0, 0).wait()
        weave(each_block(project, keys, w_key, (0, 0)))
        for which in range(1, len(sources)):
            arrival(which, 0).wait()
        weave(both_heads(score, (0, 0)), each_block(project, keys, w_key, (0, 1)))
        weave(each_block(project, values, w_value, (0, 0)))

        def two_turns(group, carry):
            for which in range(len(sources)):
                arrival(which, group + 1).wait()

            @pl.when(group > 0)
            def _():
                depart(group - 1)

            turn((group, 0), (group, 1), (group + 1, 0))
            turn((group, 1), (group + 1, 0), (group + 1, 1))
            return carry

        lax.fori_loop(0, groups - 1, two_turns, 0)
        if groups > 1:
            depart(groups - 2)
        turn((groups - 1, 0), (groups - 1, 1), None)
        turn((groups - 1, 1), None, None)
        depart(groups - 1)

    if first or blocks < 3:
        work(tok, blocks)
    else:
        first_query = place[0] * tok
        doc_start = doc_stop = before = jnp.int32(0)
        for doc in range(lengths.shape[0]):
            after = before + lengths[doc]
            here = (before <= first_query) & (first_query < after)
            doc_start = jnp.where(here, before, doc_start)
            doc_stop = jnp.where(here, after, doc_stop)
            before = after
        few = doc_stop - first_query <= tok // 2
        near_enough = first_query - doc_start <= (WINDOW - 2) * tok
        pl.when(few)(lambda: work(tok // 2, blocks))
        if last:
            pl.when(jnp.logical_not(few) & near_enough)(lambda: work(tok, blocks - 1))
            pl.when(jnp.logical_not(few | near_enough))(lambda: work(tok, blocks))
        else:
            pl.when(jnp.logical_not(few))(lambda: work(tok, blocks))
    for group in range(groups):
        for which in range(len(targets)):
            departure(which, group).wait()


def part_rows_of(packed_shape, width, rope):
    return packed_shape[1] * width // (width + rope)


def attend(lengths, halves, material, pieces, q_nope, q_rope, w_key, w_value, state, diagonal, last):
    tok, wide = q_nope.shape
    groups = wide // HEAD_DIM // 4
    width = w_key.shape[0]
    rope = q_rope.shape[1] * HEAD_DIM // wide
    span = len(pieces) * part_rows_of(material[0].shape, width, rope)
    any_ = pl.BlockSpec(memory_space=pl.ANY)
    sources = [w_key, q_nope, q_rope, w_value, *state]
    if last:
        out_shape = [jax.ShapeDtypeStruct((tok, wide), bf16)]
    else:
        out_shape = [
            jax.ShapeDtypeStruct((tok, wide), f32),
            jax.ShapeDtypeStruct((groups, tok, 128), f32),
        ]
    by_group = lambda x: pltpu.VMEM(
        (groups, x.shape[-2], x.shape[-1] // (groups if len(x.shape) == 2 else 1)), x.dtype
    )
    flops = 2 * span * wide * (2 * width + 4 * tok)
    return pl.pallas_call(
        functools.partial(attend_kernel, (pieces, len(material), halves, diagonal, not state, last)),
        in_specs=[pl.BlockSpec(memory_space=pltpu.SMEM)]
        + [pl.BlockSpec(memory_space=pltpu.VMEM)] * len(material) + [any_] * len(sources),
        out_specs=[any_] * len(out_shape),
        out_shape=out_shape,
        scratch_shapes=[by_group(x) for x in sources + out_shape]
        + [
            pltpu.VMEM((2, span, 256), bf16),
            pltpu.VMEM((2, span, 256), bf16),
            pltpu.VMEM((2, 2, tok, span), f32),
            pltpu.VMEM((2, 2, tok, span), bf16),
            pltpu.VMEM((2, 2, tok, 128), f32),
            pltpu.VMEM((2, 2, tok, 128), f32),
            pltpu.VMEM((2, span, 128), bf16),
            pltpu.VMEM((tok, 128), bf16),
            pltpu.VMEM((tok, tok), f32),
            pltpu.SemaphoreType.DMA((len(material),)),
            pltpu.SemaphoreType.DMA((len(sources), groups)),
            pltpu.SemaphoreType.DMA((len(out_shape), groups)),
        ],
        compiler_params=pltpu.CompilerParams(vmem_limit_bytes=60 << 20),
        cost_estimate=pl.CostEstimate(
            flops=flops, bytes_accessed=16 << 20, transcendentals=tok * span * wide // HEAD_DIM
        ),
    )(lengths, *material, *sources)


def shards(q_nope, q_rope, latents, rope_keys, doc_lengths, w_key, w_value):
    halves = lax.axis_size("head") == 2
    if halves:
        swap = lambda x: lax.ppermute(x, "head", [(0, 1), (1, 0)])
    else:
        latents = lax.all_gather(latents, "head", axis=0, tiled=True)
        rope_keys = lax.all_gather(rope_keys, "head", axis=1, tiled=True)
    run = lambda material, pieces, state, last: attend(
        doc_lengths, halves, material, pieces, q_nope, q_rope, w_key, w_value, state, not state, last
    )
    own = pack(latents, rope_keys)
    near = [from_behind(own, by) for by in (1, 2, 3)]
    if halves:
        state = run([own[None], swap(own[None])], [(0, 0, 0, False), (1, 0, 0, True)], (), False)
    else:
        state = run([own[None]], [(0, 0, 0, False)], (), False)
    near, state = lax.optimization_barrier((near, state))
    near = jnp.stack(near)
    far = from_behind(jnp.concatenate([own[None], near]), 4)
    whose = (False, True) if halves else (False,)
    near_pieces = [(int(other), at - 1, at, other) for at in (1, 2, 3) for other in whose]
    far_pieces = [(int(other), at - 4, at, other) for at in (4, 5, 6, 7) for other in whose]
    if halves:
        both = lambda x: [x, swap(x)]
    else:
        both = lambda x: [x]
    state = run(both(near), near_pieces, state, False)
    far, state = lax.optimization_barrier((far, state))
    return run(both(far), far_pieces, state, True)[0]


def solution(mesh):
    return jax.shard_map(
        shards,
        mesh=mesh,
        in_specs=(
            P("ctx", "head"),
            P("ctx", "head"),
            P(("ctx", "head"), None),
            P(None, ("ctx", "head")),
            P(),
            P(None, "head"),
            P(None, "head"),
        ),
        out_specs=P("ctx", "head"),
        check_vma=False,
    )
```

```python
import functools
import math

import jax
import jax.numpy as jnp
from jax import lax
from jax.experimental import pallas as pl
from jax.experimental.pallas import tpu as pltpu
from jax.sharding import PartitionSpec as P

HEAD_DIM = 128
WINDOW = 8

masked_score = -1e30
f32, bf16 = jnp.float32, jnp.bfloat16
NT = (((1,), (1,)), ((), ()))


def from_behind(x, by):
    length = lax.axis_size("ctx")
    return lax.ppermute(x, "ctx", [(i, (i + by) % length) for i in range(length)])


def pack_kernel(latents, rope_keys, packed):
    rows = latents.shape[0]
    packed[:rows, :] = latents[...]
    lanes = rope_keys.shape[1]
    pieces = latents.shape[1] // lanes
    tall = rope_keys.shape[0] // pieces
    for piece in range(pieces):
        packed[rows:, piece * lanes : (piece + 1) * lanes] = rope_keys[
            piece * tall : (piece + 1) * tall, :
        ]


def pack(latents, rope_keys):
    rows, width = latents.shape
    below = rope_keys.size // width
    return pl.pallas_call(
        pack_kernel, out_shape=jax.ShapeDtypeStruct((rows + below, width), bf16)
    )(latents, rope_keys)


def weave(*lists):
    calls = [((at + 0.5) / len(each), turn, call) for turn, each in enumerate(lists) for at, call in enumerate(each)]
    for _, _, call in sorted(calls, key=lambda entry: entry[:2]):
        call()


def attend_kernel(shape, *refs):
    pieces, arrays, halves, diagonal, first, last = shape
    lengths = refs[0]
    rest = list(refs[1:])
    place = (lax.axis_index("ctx"), lax.axis_index("head") if halves else 0)
    take = lambda count: [rest.pop(0) for _ in range(count)]
    packed = take(arrays)
    sources = take(4 if first else 6)
    targets = take(1 if last else 2)
    material = packed
    landed = take(len(sources))
    leaving = take(len(targets))
    keys, values, scores_of, weights_of, tops, fades, side, query_side, later, unpacked, came, went = take(12)
    w_key, q_nope, q_rope, w_value = landed[:4]
    tok = q_nope.shape[1]
    groups = q_nope.shape[0]
    part_rows = part_rows_of(packed[0].shape, w_key.shape[1], q_rope.shape[2] // 4)
    span = len(pieces) * part_rows
    bounds = [(at, min(at + tok, span)) for at in range(0, span, tok)]
    blocks = len(bounds)
    width = w_key.shape[1]
    rope = q_rope.shape[2] // 4
    scale = math.log2(math.e) / math.sqrt(HEAD_DIM + rope)
    lane = lax.broadcasted_iota(jnp.int32, (tok, 128), 1)
    low = lane < 64

    def columns_of(ref, group, wide):
        if len(ref.shape) == 3:
            return ref.at[group]
        start = group * wide
        return ref.at[:, pl.ds(start if isinstance(start, int) else pl.multiple_of(start, wide), wide)]

    def arrival(which, group):
        into = landed[which].at[group]
        return pltpu.make_async_copy(
            columns_of(sources[which], group, into.shape[-1]), into, came.at[which, group]
        )

    def departure(which, group):
        from_ = leaving[which].at[group]
        return pltpu.make_async_copy(
            from_, columns_of(targets[which], group, from_.shape[-1]), went.at[which, group]
        )

    for which in range(len(sources)):
        arrival(which, 0).start()
    early = groups if first else min(2, groups)
    for group in range(1, early):
        for which in range(len(sources)):
            arrival(which, group).start()

    def depart(group):
        for which in range(len(targets)):
            departure(which, group).start()

    at = lax.broadcasted_iota(jnp.int32, (8, 128), 1) % 64
    start, stop = jnp.zeros((8, 128), jnp.int32), jnp.zeros((8, 128), jnp.int32)
    before = jnp.int32(0)
    for doc in range(lengths.shape[0]):
        after = before + lengths[doc]
        start = jnp.where(at == doc, before, start)
        stop = jnp.where(at == doc, after, stop)
        before = after
    start, stop = start[:1], stop[:1]
    row = lax.broadcasted_iota(jnp.int32, (tok, 128), 0)
    position = place[0] * tok + row
    inside = (position >= start) & (position < stop)
    query_side[...] = jnp.where(inside, 1.0, 0.0).astype(bf16)

    def turned(at):
        at = at + place[1] * part_rows
        return jnp.where(at >= tok, at - tok, at)

    if diagonal:
        query_at = lax.broadcasted_iota(jnp.int32, (tok, tok), 0)
        key_at = turned(lax.broadcasted_iota(jnp.int32, (tok, tok), 1))
        later[...] = jnp.where(key_at <= query_at, 0.0, masked_score)
    folds = width // part_rows
    row = lax.broadcasted_iota(jnp.int32, (part_rows, 128), 0)
    low_rows = lax.broadcasted_iota(jnp.int32, (part_rows, 128), 1) < 64
    for at, (array, index, distance, other) in enumerate(pieces):
        part = 1 - place[1] if other else place[1]
        position = (place[0] - distance) * tok + part * part_rows + row
        inside = (position >= start) & (position < stop)
        elsewhere = jnp.where(inside, 0.0, masked_score)
        folded = material[array][index, part_rows:, :].astype(f32)
        flat = jnp.concatenate(
            [folded[:, p * part_rows : (p + 1) * part_rows] for p in range(folds)] * 2, axis=0
        )
        rotary = flat.T
        rows = slice(at * part_rows, (at + 1) * part_rows)
        side[0, rows, :] = jnp.where(low_rows, rotary, elsewhere).astype(bf16)
        side[1, rows, :] = jnp.where(low_rows, elsewhere, rotary).astype(bf16)

    def latents(block):
        low_end, high_end = (bound // part_rows for bound in bounds[block])
        return jnp.concatenate(
            [material[array][index, :part_rows, :] for array, index, _, _ in pieces[low_end:high_end]],
            axis=0,
        )

    def work(tall, blocks):
        reach = bounds[blocks - 1][1]

        def project(into, weight, pair, block):
            group, half = pair
            rows = slice(*bounds[block])
            columns = slice(half * 256, (half + 1) * 256)
            into[half, rows, :] = jnp.dot(
                latents(block), weight[group, :, columns], preferred_element_type=f32
            ).astype(bf16)

        queries = {}

        def score(pair, odd, block):
            group, half = pair
            rows = slice(*bounds[block])
            columns = slice(odd * HEAD_DIM, (odd + 1) * HEAD_DIM)
            head = slice((2 * half + odd) * HEAD_DIM, (2 * half + odd + 1) * HEAD_DIM)
            if block == 0:
                rotary = q_rope[group, :tall, half * 128 : (half + 1) * 128]
                queries[0] = jnp.concatenate(
                    [q_nope[group, :tall, head], jnp.where(low[:tall] != (odd == 1), rotary, query_side[:tall, :])],
                        axis=1,
                )
            key = jnp.concatenate([keys[half, rows, columns], side[odd, rows, :]], axis=1)
            scores = lax.dot_general(queries[0], key, NT, preferred_element_type=f32)
            if diagonal and block == 0:
                scores = scores + later[...]
            scores_of[half, odd, :tall, rows] = scores
            top = functools.reduce(
                jnp.maximum, [scores[:, at : at + 128] for at in range(0, scores.shape[1], 128)]
            )
            queries["top"] = top if block == 0 else jnp.maximum(queries["top"], top)
            if block == blocks - 1:
                top = jnp.max(queries["top"], axis=1, keepdims=True) * scale
                if not first:
                    lane_at = 4 * half + odd
                    earlier = landed[5][group, :tall, lane_at : lane_at + 1]
                    top = jnp.maximum(top, earlier)
                    fades[half, odd, :tall] = jnp.broadcast_to(jnp.exp2(earlier - top), (tall, 128))
                tops[half, odd, :tall] = jnp.broadcast_to(top, (tall, 128))

        def raise_(pair, odd, block):
            group, half = pair
            rows = slice(*bounds[block])
            top = jnp.concatenate([tops[half, odd, :tall]] * ((rows.stop - rows.start) // 128), axis=1)
            raised = jnp.exp2(scores_of[half, odd, :tall, rows] * scale - top)
            weights_of[half, odd, :tall, rows] = raised.astype(bf16)

        def mix(pair, odd):
            group, half = pair
            columns = slice(odd * HEAD_DIM, (odd + 1) * HEAD_DIM)
            head = slice((2 * half + odd) * HEAD_DIM, (2 * half + odd + 1) * HEAD_DIM)
            value = jnp.concatenate(
                [values[half, :reach, columns], jnp.ones((reach, 128), bf16)], axis=1
            )
            mixed = jnp.dot(weights_of[half, odd, :tall, :reach], value, preferred_element_type=f32)
            mixed, denom = mixed[:, :128], mixed[:, 128:]
            if not first:
                fade = fades[half, odd, :tall]
                mixed = mixed + landed[4][group, :tall, head] * fade
                lane_at = 4 * half + 2 + odd
                denom = denom + landed[5][group, :tall, lane_at : lane_at + 1] * fade
            if last:
                mixed = mixed / denom
            else:
                stat = leaving[1][group, :tall]
                stat = jnp.where(lane[:tall] == 4 * half + odd, tops[half, odd, :tall], stat)
                stat = jnp.where(lane[:tall] == 4 * half + 2 + odd, denom, stat)
                leaving[1][group, :tall] = stat
            leaving[0][group, :tall, head] = mixed.astype(leaving[0].dtype)
            if tall < tok:
                others = landed[4][group, tall:, head]
                if last:
                    others = others / landed[5][group, tall:, lane_at : lane_at + 1]
                elif odd == 1:
                    stat = landed[5][group, tall:]
                    pair_lanes = (lane[tall:] >= 4 * half) & (lane[tall:] < 4 * half + 4)
                    leaving[1][group, tall:] = jnp.where(pair_lanes, stat, leaving[1][group, tall:])
                leaving[0][group, tall:, head] = others.astype(leaving[0].dtype)

        def each_block(call, *args):
            return [functools.partial(call, *args, block) for block in range(blocks)]

        def both_heads(call, pair):
            return each_block(call, pair, 0) + each_block(call, pair, 1)

        def turn(mixed, scored, keyed):
            raises = both_heads(raise_, mixed)
            half = len(raises) // 2 if keyed else len(raises)
            if scored:
                weave(both_heads(score, scored), raises[:half])
            else:
                weave(raises[:half])
            if keyed:
                weave(each_block(project, keys, w_key, keyed), raises[half:])
            mix(mixed, 0)
            mix(mixed, 1)
            if scored:
                weave(each_block(project, values, w_value, scored))

        arrival(0, 0).wait()
        for group in range(early, groups):
            for which in range(len(sources)):
                arrival(which, group).start()
        weave(each_block(project, keys, w_key, (0, 0)))
        for which in range(1, len(sources)):
            arrival(which, 0).wait()
        weave(both_heads(score, (0, 0)), each_block(project, keys, w_key, (0, 1)))
        weave(each_block(project, values, w_value, (0, 0)))

        def two_turns(group, carry):
            for which in range(len(sources)):
                arrival(which, group + 1).wait()

            @pl.when(group > 0)
            def _():
                depart(group - 1)

            turn((group, 0), (group, 1), (group + 1, 0))
            turn((group, 1), (group + 1, 0), (group + 1, 1))
            return carry

        lax.fori_loop(0, groups - 1, two_turns, 0)
        if groups > 1:
            depart(groups - 2)
        turn((groups - 1, 0), (groups - 1, 1), None)
        turn((groups - 1, 1), None, None)
        depart(groups - 1)

    if first or blocks < 3:
        work(tok, blocks)
    else:
        first_query = place[0] * tok
        doc_start = doc_stop = before = jnp.int32(0)
        for doc in range(lengths.shape[0]):
            after = before + lengths[doc]
            here = (before <= first_query) & (first_query < after)
            doc_start = jnp.where(here, before, doc_start)
            doc_stop = jnp.where(here, after, doc_stop)
            before = after
        few = doc_stop - first_query <= tok // 2
        near_enough = first_query - doc_start <= (WINDOW - 2) * tok
        pl.when(few)(lambda: work(tok // 2, blocks))
        if last:
            pl.when(jnp.logical_not(few) & near_enough)(lambda: work(tok, blocks - 1))
            pl.when(jnp.logical_not(few | near_enough))(lambda: work(tok, blocks))
        else:
            pl.when(jnp.logical_not(few))(lambda: work(tok, blocks))
    for group in range(groups):
        for which in range(len(targets)):
            departure(which, group).wait()


def part_rows_of(packed_shape, width, rope):
    return packed_shape[1] * width // (width + rope)


def attend(lengths, halves, material, pieces, q_nope, q_rope, w_key, w_value, state, diagonal, last):
    tok, wide = q_nope.shape
    groups = wide // HEAD_DIM // 4
    width = w_key.shape[0]
    rope = q_rope.shape[1] * HEAD_DIM // wide
    span = len(pieces) * part_rows_of(material[0].shape, width, rope)
    any_ = pl.BlockSpec(memory_space=pl.ANY)
    sources = [w_key, q_nope, q_rope, w_value, *state]
    if last:
        out_shape = [jax.ShapeDtypeStruct((tok, wide), bf16)]
    else:
        out_shape = [
            jax.ShapeDtypeStruct((tok, wide), f32),
            jax.ShapeDtypeStruct((groups, tok, 128), f32),
        ]
    by_group = lambda x: pltpu.VMEM(
        (groups, x.shape[-2], x.shape[-1] // (groups if len(x.shape) == 2 else 1)), x.dtype
    )
    flops = 2 * span * wide * (2 * width + 4 * tok)
    return pl.pallas_call(
        functools.partial(attend_kernel, (pieces, len(material), halves, diagonal, not state, last)),
        in_specs=[pl.BlockSpec(memory_space=pltpu.SMEM)]
        + [pl.BlockSpec(memory_space=pltpu.VMEM)] * len(material) + [any_] * len(sources),
        out_specs=[any_] * len(out_shape),
        out_shape=out_shape,
        scratch_shapes=[by_group(x) for x in sources + out_shape]
        + [
            pltpu.VMEM((2, span, 256), bf16),
            pltpu.VMEM((2, span, 256), bf16),
            pltpu.VMEM((2, 2, tok, span), f32),
            pltpu.VMEM((2, 2, tok, span), bf16),
            pltpu.VMEM((2, 2, tok, 128), f32),
            pltpu.VMEM((2, 2, tok, 128), f32),
            pltpu.VMEM((2, span, 128), bf16),
            pltpu.VMEM((tok, 128), bf16),
            pltpu.VMEM((tok, tok), f32),
            pltpu.SemaphoreType.DMA((len(material),)),
            pltpu.SemaphoreType.DMA((len(sources), groups)),
            pltpu.SemaphoreType.DMA((len(out_shape), groups)),
        ],
        compiler_params=pltpu.CompilerParams(vmem_limit_bytes=60 << 20),
        cost_estimate=pl.CostEstimate(
            flops=flops, bytes_accessed=16 << 20, transcendentals=tok * span * wide // HEAD_DIM
        ),
    )(lengths, *material, *sources)


def shards(q_nope, q_rope, latents, rope_keys, doc_lengths, w_key, w_value):
    halves = lax.axis_size("head") == 2
    if halves:
        swap = lambda x: lax.ppermute(x, "head", [(0, 1), (1, 0)])
    else:
        latents = lax.all_gather(latents, "head", axis=0, tiled=True)
        rope_keys = lax.all_gather(rope_keys, "head", axis=1, tiled=True)
    run = lambda material, pieces, state, last: attend(
        doc_lengths, halves, material, pieces, q_nope, q_rope, w_key, w_value, state, not state, last
    )
    own = pack(latents, rope_keys)
    near = [from_behind(own, by) for by in (1, 2, 3)]
    if halves:
        state = run([own[None], swap(own[None])], [(0, 0, 0, False), (1, 0, 0, True)], (), False)
    else:
        state = run([own[None]], [(0, 0, 0, False)], (), False)
    near, state = lax.optimization_barrier((near, state))
    near = jnp.stack(near)
    far = from_behind(jnp.concatenate([own[None], near]), 4)
    whose = (False, True) if halves else (False,)
    near_pieces = [(int(other), at - 1, at, other) for at in (1, 2, 3) for other in whose]
    far_pieces = [(int(other), at - 4, at, other) for at in (4, 5, 6, 7) for other in whose]
    if halves:
        both = lambda x: [x, swap(x)]
    else:
        both = lambda x: [x]
    state = run(both(near), near_pieces, state, False)
    far, state = lax.optimization_barrier((far, state))
    return run(both(far), far_pieces, state, True)[0]


def solution(mesh):
    return jax.shard_map(
        shards,
        mesh=mesh,
        in_specs=(
            P("ctx", "head"),
            P("ctx", "head"),
            P(("ctx", "head"), None),
            P(None, ("ctx", "head")),
            P(),
            P(None, "head"),
            P(None, "head"),
        ),
        out_specs=P("ctx", "head"),
        check_vma=False,
    )
```
